32 devices in a mesh: rep: 16 (over z, y, core), fsdp: 2 (over x).
Axes of the slice: x: 2, y: 2, z: 4, core: 2. Of those that a mesh axis runs over, the one named last changes fastest.
Arguments:
- weights: bfloat16 [16, 2048, 512], P('rep', 'fsdp'), may hold values from -0.125 to 0.125
- first_moment: float32 [16, 2048, 512], P('rep', 'fsdp'), may hold values from -120 to 120
- second_moment: float32 [16, 2048, 512], P('rep', 'fsdp'), may hold values from 25 to 2500
- layer_inputs: bfloat16 [7168, 2048], P(('rep', 'fsdp')), may hold values from -6 to 6
- output_grad: bfloat16 [7168, 512], P(('rep', 'fsdp')), may hold values from -3 to 3
- next_inputs: bfloat16 [7168, 2048], P(('rep', 'fsdp')), may hold values from -6 to 6
- step_index: int32 [1], replicated, may hold values from 0 to 999
Outputs:
- input_grad: bfloat16 [7168, 2048], P(('rep', 'fsdp'))
- next_outputs: bfloat16 [7168, 512], P(('rep', 'fsdp'))
- new_moment: float32 [16, 2048, 512], P('rep', 'fsdp')
The draws below stay inside these ranges and needn't reach their ends.
Inputs may be any that keep to these rules, and one draw needn't show every extreme that they name: step_index selects the partner offset through its remainder modulo floor(log2(16)) and sets the bias corrections.
All inputs are finite; a program needn't handle non-finite values.
Results may differ from the reference program's by a relative error of at most 0.0045.
The reference program's roundings to bfloat16 on the way (of `updated` and `averaged`) count: a program that leaves them out, or rounds other values in their place, can miss the bound.
Values may be sent and summed in bfloat16 or wider, within the bound.
A program may use at most 64 MiB of HBM per device.

```python
import math
import jax
import jax.numpy as jnp
from jax import lax

D_IN = 2048
KV = 512
TOKENS = 7168
N_REP = 16


def level_of(own_key, extent, shards, low, high):
    level = 1.0
    for dim, shards_of in shards:
        heights = jax.random.uniform(jax.random.fold_in(jax.random.fold_in(own_key, 6), dim), (shards_of,), jnp.float32, low / len(shards), high / len(shards))
        level = level * jnp.repeat(jnp.exp(heights), extent[dim] // shards_of).reshape((-1,) + (1,) * (len(extent) - 1 - dim))
    return level


def scatter_about(own_key, shape, deviation, bound, pieces=(), kind=jnp.bfloat16):
    gain = level_of(own_key, shape, pieces, -0.22, 0.18) if pieces else 1.0
    drawn = jax.random.normal(own_key, shape, jnp.float32) * deviation * gain
    return jnp.minimum(jnp.maximum(drawn, -bound), bound).astype(kind)


def setup_inputs(seed: int = 0) -> dict:
    splits = jax.random.split(jax.random.key(seed), 8)
    return {
        "weights": scatter_about(splits[0], (N_REP, D_IN, KV), D_IN ** -0.5, 0.125, ((0, 16), (1, 2))),
        "first_moment": scatter_about(splits[1], (N_REP, D_IN, KV), 20.0, 120.0, ((0, 16), (1, 2)), jnp.float32),
        "second_moment": jnp.clip(jnp.exp(math.log(2500.0) - 4.6051702 * jax.random.uniform(splits[2], (N_REP, D_IN, KV), jnp.float32) ** level_of(splits[2], (N_REP, D_IN, KV), ((0, 16), (1, 2)), -0.2, 0.2)), 25.0, 2500.0),
        "layer_inputs": scatter_about(splits[3], (TOKENS, D_IN), 1.0, 6.0, ((0, 32),)),
        "output_grad": scatter_about(splits[4], (TOKENS, KV), 0.5, 3.0, ((0, 32),)),
        "next_inputs": scatter_about(splits[5], (TOKENS, D_IN), 1.0, 6.0, ((0, 32),)),
        "step_index": jax.random.randint(splits[6], (1,), 0, 1000).astype(jnp.int32),
    }


learning_rate = 0.004
beta_one = 0.9
beta_two = 0.95
adam_eps = 1e-08

def reference(weights, first_moment, second_moment, layer_inputs, output_grad, next_inputs, step_index):
    tokens = layer_inputs.reshape(N_REP, -1, D_IN)
    cotangents = output_grad.reshape(N_REP, -1, KV)
    upcoming = next_inputs.reshape(N_REP, -1, D_IN)

    def replica_backward(item):
        inputs_here, cot_here, weights_here = item
        back = jnp.dot(cot_here, weights_here.T, preferred_element_type=jnp.float32).astype(jnp.bfloat16)
        gradient = jnp.dot(inputs_here.T, cot_here, preferred_element_type=jnp.float32)
        return (back, gradient)
    back_all, gradient = lax.map(replica_backward, (tokens, cotangents, weights))
    new_moment = beta_one * first_moment + (1.0 - beta_one) * gradient
    second = beta_two * second_moment + (1.0 - beta_two) * gradient * gradient
    count = (step_index[0] + 1).astype(jnp.float32)
    fix_one = 1.0 - jnp.power(jnp.float32(beta_one), count)
    fix_two = 1.0 - jnp.power(jnp.float32(beta_two), count)
    update = learning_rate * (new_moment / fix_one) / (jnp.sqrt(second / fix_two) + adam_eps)
    updated = (weights.astype(jnp.float32) - update).astype(jnp.bfloat16)
    updated = lax.optimization_barrier(updated)
    levels = N_REP.bit_length() - 1
    offset = jnp.left_shift(jnp.int32(1), (step_index[0] % levels).astype(jnp.int32))
    received = jnp.roll(updated, offset, axis=0)
    averaged = (0.5 * (updated.astype(jnp.float32) + received.astype(jnp.float32))).astype(jnp.bfloat16)

    def replica_forward(item):
        inputs_here, matrix_here = item
        return jnp.dot(inputs_here, matrix_here, preferred_element_type=jnp.float32).astype(jnp.bfloat16)
    next_outputs = lax.map(replica_forward, (upcoming, averaged))
    return (back_all.reshape(-1, D_IN), next_outputs.reshape(-1, KV), new_moment)
```

```python
import functools
import math

import jax
import jax.numpy as jnp
from jax import lax
from jax.experimental import pallas as pl
from jax.experimental.pallas import tpu as pltpu
from jax.sharding import PartitionSpec as P

learning_rate = 0.004
beta_one = 0.9
beta_two = 0.95
adam_eps = 1e-08
MESH = pl.DeviceIdType.MESH
BF16, F32 = jnp.bfloat16, jnp.float32


def step_kernel(
    offset, reps, shards, chunk, step_ref, w_hbm, m_hbm, v_hbm, li_hbm, og_hbm, ni_hbm,
    ig_hbm, no_hbm, nm_hbm,
    w, m, v, li, og, ni, grad, upd, got, ig, acc, sent, part, no,
    load_sem, og_sem, ni_sem, out_sem, nm_sem, ig_out_sem, og_send, og_recv, li_send, li_recv,
    ni_send, ni_recv, ig_send, ig_recv, rep_send, rep_recv, part_send, part_recv,
):
    rep, shard = lax.axis_index("rep"), lax.axis_index("fsdp")
    tokens, width = og_hbm.shape
    rows = w_hbm.shape[1]
    chunks = rows // chunk
    peers = range(1, shards)

    def ahead(s):
        return lax.rem(shard + s, shards)

    def behind(s):
        return lax.rem(shard + shards - s, shards)

    def columns(owner, c):
        return pl.ds(pl.multiple_of(owner * rows + c * chunk, chunk), chunk)

    def rows_of(c):
        return pl.ds(pl.multiple_of(c * chunk, chunk), chunk)

    def slot(s):
        return pl.ds(s * tokens, tokens)

    def og_load():
        return pltpu.make_async_copy(og_hbm, og.at[slot(0)], og_sem)

    def loads(c):
        return [
            pltpu.make_async_copy(li_hbm.at[:, columns(shard, c)], li.at[c, slot(0)], load_sem.at[0, c]),
            pltpu.make_async_copy(w_hbm.at[0, rows_of(c)], w.at[c], load_sem.at[1, c]),
            pltpu.make_async_copy(m_hbm.at[0, rows_of(c)], m.at[c], load_sem.at[2, c]),
            pltpu.make_async_copy(v_hbm.at[0, rows_of(c)], v.at[c], load_sem.at[3, c]),
        ]

    def ni_load(c):
        return pltpu.make_async_copy(ni_hbm.at[:, columns(shard, c)], ni.at[c, slot(0)], ni_sem.at[c])

    def og_move(s):
        return pltpu.make_async_remote_copy(
            og_hbm, og.at[slot(s)], og_send.at[s], og_recv.at[s],
            device_id=(rep, ahead(s)), device_id_type=MESH)

    def li_move(s, c):
        return pltpu.make_async_remote_copy(
            li_hbm.at[:, columns(ahead(s), c)], li.at[c, slot(s)], li_send.at[s, c], li_recv.at[s, c],
            device_id=(rep, ahead(s)), device_id_type=MESH)

    def ni_move(s, c):
        return pltpu.make_async_remote_copy(
            ni_hbm.at[:, columns(ahead(s), c)], ni.at[c, slot(s)], ni_send.at[s, c], ni_recv.at[s, c],
            device_id=(rep, ahead(s)), device_id_type=MESH)

    def ig_move(s, c):
        return pltpu.make_async_remote_copy(
            ig.at[c, slot(s)], ig_hbm.at[:, columns(shard, c)], ig_send.at[s, c], ig_recv.at[s, c],
            device_id=(rep, behind(s)), device_id_type=MESH)

    def ig_store(c):
        return pltpu.make_async_copy(ig.at[c, slot(0)], ig_hbm.at[:, columns(shard, c)], ig_out_sem.at[c])

    def rep_move(c):
        return pltpu.make_async_remote_copy(
            upd.at[c], got.at[c], rep_send.at[c], rep_recv.at[c],
            device_id=(lax.rem(rep + offset, reps), shard), device_id_type=MESH)

    def nm_store(c):
        return pltpu.make_async_copy(m.at[c], nm_hbm.at[0, rows_of(c)], nm_sem.at[c])

    def part_move(s):
        return pltpu.make_async_remote_copy(
            sent.at[s - 1], part.at[s - 1], part_send.at[s], part_recv.at[s],
            device_id=(rep, behind(s)), device_id_type=MESH)

    barrier = pltpu.get_barrier_semaphore()
    greeted = [(rep, ahead(s)) for s in peers]
    greeted.append((lax.rem(rep + offset, reps), shard))
    if 2 * offset != reps:
        greeted.append((lax.rem(rep + reps - offset, reps), shard))
    for other in greeted:
        pl.semaphore_signal(barrier, inc=1, device_id=other, device_id_type=MESH)
    og_load().start()
    for c in range(chunks):
        for copy in loads(c):
            copy.start()
    for c in range(chunks):
        ni_load(c).start()
    pl.semaphore_wait(barrier, len(greeted))
    for s in peers:
        og_move(s).start()
    for c in range(chunks):
        for s in peers:
            li_move(s, c).start()

    count = jnp.full((1, width), (step_ref[0] + 1).astype(F32))
    scale_one = learning_rate / (1.0 - jnp.exp(count * math.log(beta_one)))
    scale_two = 1.0 / (1.0 - jnp.exp(count * math.log(beta_two)))

    og_load().wait()
    for s in peers:
        og_move(s).wait_recv()

    block = 32

    @pl.loop(0, chunks)
    def _(c):
        for copy in loads(c):
            copy.wait()
        for s in peers:
            li_move(s, c).wait_recv()
        grad[...] = lax.dot_general(
            li[c], og[...], (((0,), (0,)), ((), ())), preferred_element_type=F32)

        @pl.loop(0, chunk // block)
        def _(b):
            here = pl.ds(pl.multiple_of(b * block, block), block)
            g = grad[here]
            moment = beta_one * m[c, here] + (1.0 - beta_one) * g
            second = beta_two * v[c, here] + (1.0 - beta_two) * g * g
            m[c, here] = moment
            update = (moment * scale_one) / (jnp.sqrt(second * scale_two) + adam_eps)
            upd[c, here] = (w[c, here].astype(F32) - update).astype(BF16)

        rep_move(c).start()
        nm_store(c).start()

    for c in range(chunks):
        for s in peers:
            ni_move(s, c).start()

    @pl.loop(0, chunks)
    def _(c):
        ig[c] = lax.dot_general(
            og[...], w[c], (((1,), (1,)), ((), ())), preferred_element_type=F32).astype(BF16)
        for s in peers:
            ig_move(s, c).start()
        ig_store(c).start()

    acc[...] = jnp.zeros_like(acc)
    travelling = pl.ds(tokens, (shards - 1) * tokens)

    @pl.loop(0, chunks)
    def _(c):
        ni_load(c).wait()
        for s in peers:
            ni_move(s, c).wait_recv()
        rep_move(c).wait_recv()

        @pl.loop(0, chunk // block)
        def _(b):
            here = pl.ds(pl.multiple_of(b * block, block), block)
            got[c, here] = (0.5 * (upd[c, here].astype(F32) + got[c, here].astype(F32))).astype(BF16)

        if shards > 1:
            acc[travelling] += jnp.dot(ni[c, travelling], got[c], preferred_element_type=F32)

    for s in peers:
        sent[s - 1] = acc[slot(s)].astype(BF16)
        part_move(s).start()

    @pl.loop(0, chunks)
    def _(c):
        acc[slot(0)] += jnp.dot(ni[c, slot(0)], got[c], preferred_element_type=F32)

    total = acc[slot(0)]
    for s in peers:
        part_move(s).wait_recv()
        total = total + part[s - 1].astype(F32)
    no[...] = total.astype(BF16)
    no_store = pltpu.make_async_copy(no, no_hbm, out_sem)
    no_store.start()

    for s in peers:
        og_move(s).wait_send()
        part_move(s).wait_send()
    for c in range(chunks):
        for s in peers:
            li_move(s, c).wait_send()
            ni_move(s, c).wait_send()
            ig_move(s, c).wait_send()
            ig_move(s, c).wait_recv()
        ig_store(c).wait()
        nm_store(c).wait()
        rep_move(c).wait_send()
    no_store.wait()


def step_call(offset, level, reps, shards, operands):
    step_index, weights, first_moment, second_moment, layer_inputs, output_grad, next_inputs = operands
    rows, width = weights.shape[1:]
    tokens, depth = layer_inputs.shape
    chunk = min(256, rows)
    chunks = rows // chunk
    whole = tokens * shards
    dma = pltpu.SemaphoreType.DMA
    anywhere = pl.BlockSpec(memory_space=pl.ANY)
    each, every = dma((shards,)), dma((shards, chunks))
    return pl.pallas_call(
        functools.partial(step_kernel, offset, reps, shards, chunk),
        out_shape=(
            jax.ShapeDtypeStruct((tokens, depth), BF16),
            jax.ShapeDtypeStruct((tokens, width), BF16),
            jax.ShapeDtypeStruct((1, rows, width), F32),
        ),
        in_specs=[pl.BlockSpec(memory_space=pltpu.SMEM)] + [anywhere] * 6,
        out_specs=(anywhere,) * 3,
        scratch_shapes=[
            pltpu.VMEM((chunks, chunk, width), BF16),
            pltpu.VMEM((chunks, chunk, width), F32),
            pltpu.VMEM((chunks, chunk, width), F32),
            pltpu.VMEM((chunks, whole, chunk), BF16),
            pltpu.VMEM((whole, width), BF16),
            pltpu.VMEM((chunks, whole, chunk), BF16),
            pltpu.VMEM((chunk, width), F32),
            pltpu.VMEM((chunks, chunk, width), BF16),
            pltpu.VMEM((chunks, chunk, width), BF16),
            pltpu.VMEM((chunks, whole, chunk), BF16),
            pltpu.VMEM((whole, width), F32),
            pltpu.VMEM((max(shards - 1, 1), tokens, width), BF16),
            pltpu.VMEM((max(shards - 1, 1), tokens, width), BF16),
            pltpu.VMEM((tokens, width), BF16),
            dma((4, chunks)), dma, dma((chunks,)), dma, dma((chunks,)), dma((chunks,)),
            each, each, every, every, every, every, every, every, dma((chunks,)), dma((chunks,)), each, each,
        ],
        compiler_params=pltpu.CompilerParams(
            collective_id=level, has_side_effects=True, vmem_limit_bytes=56 * 1024 * 1024),
        cost_estimate=pl.CostEstimate(
            flops=6 * whole * rows * width, bytes_accessed=12 * 1024 * 1024, transcendentals=rows * width),
        name=f"adam_average_{offset}",
    )(*operands)


def on_device(
    weights, first_moment, second_moment, layer_inputs, output_grad, next_inputs, step_index
):
    reps, shards = lax.axis_size("rep"), lax.axis_size("fsdp")
    levels = reps.bit_length() - 1
    operands = (step_index, weights, first_moment, second_moment, layer_inputs, output_grad, next_inputs)
    branches = [
        lambda *given, level=level: step_call(1 << level, level, reps, shards, given)
        for level in range(levels)
    ]
    return lax.switch(step_index[0] % levels, branches, *operands)


def solution(mesh):
    return jax.shard_map(
        on_device,
        mesh=mesh,
        in_specs=(
            P("rep", "fsdp", None),
            P("rep", "fsdp", None),
            P("rep", "fsdp", None),
            P(("rep", "fsdp"), None),
            P(("rep", "fsdp"), None),
            P(("rep", "fsdp"), None),
            P(),
        ),
        out_specs=(P(("rep", "fsdp"), None), P(("rep", "fsdp"), None), P("rep", "fsdp", None)),
        check_vma=False,
    )
```

```python
import functools
import math

import jax
import jax.numpy as jnp
from jax import lax
from jax.experimental import pallas as pl
from jax.experimental.pallas import tpu as pltpu
from jax.sharding import PartitionSpec as P

learning_rate = 0.004
beta_one = 0.9
beta_two = 0.95
adam_eps = 1e-08
MESH = pl.DeviceIdType.MESH
BF16, F32 = jnp.bfloat16, jnp.float32


def step_kernel(
    offset, reps, shards, chunk, step_ref, w_hbm, m_hbm, v_hbm, li_hbm, og_hbm, ni_hbm,
    ig_hbm, no_hbm, nm_hbm,
    w, m, v, li, og, ni, grad, upd, got, ig, acc, sent, part, no,
    load_sem, og_sem, ni_sem, out_sem, nm_sem, ig_out_sem, og_send, og_recv, li_send, li_recv,
    ni_send, ni_recv, ig_send, ig_recv, rep_send, rep_recv, part_send, part_recv,
):
    rep, shard = lax.axis_index("rep"), lax.axis_index("fsdp")
    tokens, width = og_hbm.shape
    rows = w_hbm.shape[1]
    chunks = rows // chunk
    peers = range(1, shards)

    def ahead(s):
        return lax.rem(shard + s, shards)

    def behind(s):
        return lax.rem(shard + shards - s, shards)

    def columns(owner, c):
        return pl.ds(pl.multiple_of(owner * rows + c * chunk, chunk), chunk)

    def rows_of(c):
        return pl.ds(pl.multiple_of(c * chunk, chunk), chunk)

    def slot(s):
        return pl.ds(s * tokens, tokens)

    def og_load():
        return pltpu.make_async_copy(og_hbm, og.at[slot(0)], og_sem)

    def load(kind, c):
        source, target = {
            "li": (lambda: li_hbm.at[:, columns(shard, c)], lambda: li.at[c, slot(0)]),
            "w": (lambda: w_hbm.at[0, rows_of(c)], lambda: w.at[c]),
            "m": (lambda: m_hbm.at[0, rows_of(c)], lambda: m.at[c]),
            "v": (lambda: v_hbm.at[0, rows_of(c)], lambda: v.at[c]),
        }[kind]
        return pltpu.make_async_copy(source(), target(), load_sem.at["li w m v".split().index(kind), c])

    def ni_load(c):
        return pltpu.make_async_copy(ni_hbm.at[:, columns(shard, c)], ni.at[c, slot(0)], ni_sem.at[c])

    def og_move(s):
        return pltpu.make_async_remote_copy(
            og_hbm, og.at[slot(s)], og_send.at[s], og_recv.at[s],
            device_id=(rep, ahead(s)), device_id_type=MESH)

    def li_move(s, c):
        return pltpu.make_async_remote_copy(
            li_hbm.at[:, columns(ahead(s), c)], li.at[c, slot(s)], li_send.at[s, c], li_recv.at[s, c],
            device_id=(rep, ahead(s)), device_id_type=MESH)

    def ni_move(s, c):
        return pltpu.make_async_remote_copy(
            ni_hbm.at[:, columns(ahead(s), c)], ni.at[c, slot(s)], ni_send.at[s, c], ni_recv.at[s, c],
            device_id=(rep, ahead(s)), device_id_type=MESH)

    def ig_move(s, c):
        return pltpu.make_async_remote_copy(
            ig.at[c, slot(s)], ig_hbm.at[:, columns(shard, c)], ig_send.at[s, c], ig_recv.at[s, c],
            device_id=(rep, behind(s)), device_id_type=MESH)

    def ig_store(c):
        return pltpu.make_async_copy(ig.at[c, slot(0)], ig_hbm.at[:, columns(shard, c)], ig_out_sem.at[c])

    def rep_move(c):
        return pltpu.make_async_remote_copy(
            upd.at[c], got.at[c], rep_send.at[c], rep_recv.at[c],
            device_id=(lax.rem(rep + offset, reps), shard), device_id_type=MESH)

    def nm_store(c):
        return pltpu.make_async_copy(m.at[c], nm_hbm.at[0, rows_of(c)], nm_sem.at[c])

    def part_move(s):
        return pltpu.make_async_remote_copy(
            sent.at[s - 1], part.at[s - 1], part_send.at[s], part_recv.at[s],
            device_id=(rep, behind(s)), device_id_type=MESH)

    barrier = pltpu.get_barrier_semaphore()
    greeted = [(rep, ahead(s)) for s in peers]
    greeted.append((lax.rem(rep + offset, reps), shard))
    if 2 * offset != reps:
        greeted.append((lax.rem(rep + reps - offset, reps), shard))
    for other in greeted:
        pl.semaphore_signal(barrier, inc=1, device_id=other, device_id_type=MESH)
    og_load().start()
    for c in range(chunks):
        for kind in ("w", "li", "m", "v"):
            load(kind, c).start()
    for c in range(chunks):
        ni_load(c).start()
    pl.semaphore_wait(barrier, len(greeted))
    for s in peers:
        og_move(s).start()
    for c in range(chunks):
        for s in peers:
            li_move(s, c).start()

    count = jnp.full((1, width), (step_ref[0] + 1).astype(F32))
    scale_one = learning_rate / (1.0 - jnp.exp(count * math.log(beta_one)))
    scale_two = 1.0 / (1.0 - jnp.exp(count * math.log(beta_two)))

    og_load().wait()
    for s in peers:
        og_move(s).wait_recv()

    @pl.loop(0, chunks)
    def _(c):
        load("w", c).wait()
        ig[c] = lax.dot_general(
            og[...], w[c], (((1,), (1,)), ((), ())), preferred_element_type=F32).astype(BF16)
        ig_store(c).start()

    block = 32

    @pl.loop(0, chunks)
    def _(c):
        for kind in ("li", "m", "v"):
            load(kind, c).wait()
        for s in peers:
            li_move(s, c).wait_recv()
            ni_move(s, c).start()
        grad[...] = lax.dot_general(
            li[c], og[...], (((0,), (0,)), ((), ())), preferred_element_type=F32)

        @pl.loop(0, chunk // block)
        def _(b):
            here = pl.ds(pl.multiple_of(b * block, block), block)
            g = grad[here]
            moment = beta_one * m[c, here] + (1.0 - beta_one) * g
            second = beta_two * v[c, here] + (1.0 - beta_two) * g * g
            m[c, here] = moment
            update = (moment * scale_one) / (jnp.sqrt(second * scale_two) + adam_eps)
            upd[c, here] = (w[c, here].astype(F32) - update).astype(BF16)

        rep_move(c).start()
        nm_store(c).start()

    for c in range(chunks):
        for s in peers:
            ig_move(s, c).start()

    acc[...] = jnp.zeros_like(acc)
    travelling = pl.ds(tokens, (shards - 1) * tokens)

    @pl.loop(0, chunks)
    def _(c):
        ni_load(c).wait()
        for s in peers:
            ni_move(s, c).wait_recv()
        rep_move(c).wait_recv()

        @pl.loop(0, chunk // block)
        def _(b):
            here = pl.ds(pl.multiple_of(b * block, block), block)
            got[c, here] = (0.5 * (upd[c, here].astype(F32) + got[c, here].astype(F32))).astype(BF16)

        if shards > 1:
            acc[travelling] += jnp.dot(ni[c, travelling], got[c], preferred_element_type=F32)

    for s in peers:
        sent[s - 1] = acc[slot(s)].astype(BF16)
        part_move(s).start()

    @pl.loop(0, chunks)
    def _(c):
        acc[slot(0)] += jnp.dot(ni[c, slot(0)], got[c], preferred_element_type=F32)

    total = acc[slot(0)]
    for s in peers:
        part_move(s).wait_recv()
        total = total + part[s - 1].astype(F32)
    no[...] = total.astype(BF16)
    no_store = pltpu.make_async_copy(no, no_hbm, out_sem)
    no_store.start()

    for s in peers:
        og_move(s).wait_send()
        part_move(s).wait_send()
    for c in range(chunks):
        for s in peers:
            li_move(s, c).wait_send()
            ni_move(s, c).wait_send()
            ig_move(s, c).wait_send()
            ig_move(s, c).wait_recv()
        ig_store(c).wait()
        nm_store(c).wait()
        rep_move(c).wait_send()
    no_store.wait()


def step_call(offset, level, reps, shards, operands):
    step_index, weights, first_moment, second_moment, layer_inputs, output_grad, next_inputs = operands
    rows, width = weights.shape[1:]
    tokens, depth = layer_inputs.shape
    chunk = min(256, rows)
    chunks = rows // chunk
    whole = tokens * shards
    dma = pltpu.SemaphoreType.DMA
    anywhere = pl.BlockSpec(memory_space=pl.ANY)
    each, every = dma((shards,)), dma((shards, chunks))
    return pl.pallas_call(
        functools.partial(step_kernel, offset, reps, shards, chunk),
        out_shape=(
            jax.ShapeDtypeStruct((tokens, depth), BF16),
            jax.ShapeDtypeStruct((tokens, width), BF16),
            jax.ShapeDtypeStruct((1, rows, width), F32),
        ),
        in_specs=[pl.BlockSpec(memory_space=pltpu.SMEM)] + [anywhere] * 6,
        out_specs=(anywhere,) * 3,
        scratch_shapes=[
            pltpu.VMEM((chunks, chunk, width), BF16),
            pltpu.VMEM((chunks, chunk, width), F32),
            pltpu.VMEM((chunks, chunk, width), F32),
            pltpu.VMEM((chunks, whole, chunk), BF16),
            pltpu.VMEM((whole, width), BF16),
            pltpu.VMEM((chunks, whole, chunk), BF16),
            pltpu.VMEM((chunk, width), F32),
            pltpu.VMEM((chunks, chunk, width), BF16),
            pltpu.VMEM((chunks, chunk, width), BF16),
            pltpu.VMEM((chunks, whole, chunk), BF16),
            pltpu.VMEM((whole, width), F32),
            pltpu.VMEM((max(shards - 1, 1), tokens, width), BF16),
            pltpu.VMEM((max(shards - 1, 1), tokens, width), BF16),
            pltpu.VMEM((tokens, width), BF16),
            dma((4, chunks)), dma, dma((chunks,)), dma, dma((chunks,)), dma((chunks,)),
            each, each, every, every, every, every, every, every, dma((chunks,)), dma((chunks,)), each, each,
        ],
        compiler_params=pltpu.CompilerParams(
            collective_id=level, has_side_effects=True, vmem_limit_bytes=56 * 1024 * 1024),
        cost_estimate=pl.CostEstimate(
            flops=6 * whole * rows * width, bytes_accessed=12 * 1024 * 1024, transcendentals=rows * width),
        name=f"adam_average_{offset}",
    )(*operands)


def on_device(
    weights, first_moment, second_moment, layer_inputs, output_grad, next_inputs, step_index
):
    reps, shards = lax.axis_size("rep"), lax.axis_size("fsdp")
    levels = reps.bit_length() - 1
    operands = (step_index, weights, first_moment, second_moment, layer_inputs, output_grad, next_inputs)
    branches = [
        lambda *given, level=level: step_call(1 << level, level, reps, shards, given)
        for level in range(levels)
    ]
    return lax.switch(step_index[0] % levels, branches, *operands)


def solution(mesh):
    return jax.shard_map(
        on_device,
        mesh=mesh,
        in_specs=(
            P("rep", "fsdp", None),
            P("rep", "fsdp", None),
            P("rep", "fsdp", None),
            P(("rep", "fsdp"), None),
            P(("rep", "fsdp"), None),
            P(("rep", "fsdp"), None),
            P(),
        ),
        out_specs=(P(("rep", "fsdp"), None), P(("rep", "fsdp"), None), P("rep", "fsdp", None)),
        check_vma=False,
    )
```

```python
import functools
import math

import jax
import jax.numpy as jnp
from jax import lax
from jax.experimental import pallas as pl
from jax.experimental.pallas import tpu as pltpu
from jax.sharding import PartitionSpec as P

learning_rate = 0.004
beta_one = 0.9
beta_two = 0.95
adam_eps = 1e-08
MESH = pl.DeviceIdType.MESH
BF16, F32 = jnp.bfloat16, jnp.float32


def step_kernel(
    offset, reps, shards, chunk, step_ref, w_hbm, m_hbm, v_hbm, li_hbm, og_hbm, ni_hbm,
    ig_hbm, no_hbm, nm_hbm,
    w, m, v, li, og, ni, grad, upd, got, ig, acc, sent, part, no,
    load_sem, og_sem, ni_sem, out_sem, nm_sem, ig_out_sem, og_send, og_recv, li_send, li_recv,
    ni_send, ni_recv, ig_send, ig_recv, rep_send, rep_recv, part_send, part_recv,
):
    rep, shard = lax.axis_index("rep"), lax.axis_index("fsdp")
    tokens, width = og_hbm.shape
    rows = w_hbm.shape[1]
    chunks = rows // chunk
    peers = range(1, shards)

    def ahead(s):
        return lax.rem(shard + s, shards)

    def behind(s):
        return lax.rem(shard + shards - s, shards)

    def columns(owner, c):
        return pl.ds(pl.multiple_of(owner * rows + c * chunk, chunk), chunk)

    def rows_of(c):
        return pl.ds(pl.multiple_of(c * chunk, chunk), chunk)

    def slot(s):
        return pl.ds(s * tokens, tokens)

    def og_load():
        return pltpu.make_async_copy(og_hbm, og.at[slot(0)], og_sem)

    def load(kind, c):
        source, target = {
            "li": (lambda: li_hbm.at[:, columns(shard, c)], lambda: li.at[c, slot(0)]),
            "w": (lambda: w_hbm.at[0, rows_of(c)], lambda: w.at[c]),
            "m": (lambda: m_hbm.at[0, rows_of(c)], lambda: m.at[c]),
            "v": (lambda: v_hbm.at[0, rows_of(c)], lambda: v.at[c]),
        }[kind]
        return pltpu.make_async_copy(source(), target(), load_sem.at["li w m v".split().index(kind), c])

    def ni_load(c):
        return pltpu.make_async_copy(ni_hbm.at[:, columns(shard, c)], ni.at[c, slot(0)], ni_sem.at[c])

    def og_move(s):
        return pltpu.make_async_remote_copy(
            og_hbm, og.at[slot(s)], og_send.at[s], og_recv.at[s],
            device_id=(rep, ahead(s)), device_id_type=MESH)

    def li_move(s, c):
        return pltpu.make_async_remote_copy(
            li_hbm.at[:, columns(ahead(s), c)], li.at[c, slot(s)], li_send.at[s, c], li_recv.at[s, c],
            device_id=(rep, ahead(s)), device_id_type=MESH)

    def ni_move(s, c):
        return pltpu.make_async_remote_copy(
            ni_hbm.at[:, columns(ahead(s), c)], ni.at[c, slot(s)], ni_send.at[s, c], ni_recv.at[s, c],
            device_id=(rep, ahead(s)), device_id_type=MESH)

    def ig_move(s, c):
        return pltpu.make_async_remote_copy(
            ig.at[c, slot(s)], ig_hbm.at[:, columns(shard, c)], ig_send.at[s, c], ig_recv.at[s, c],
            device_id=(rep, behind(s)), device_id_type=MESH)

    def ig_store(c):
        return pltpu.make_async_copy(ig.at[c, slot(0)], ig_hbm.at[:, columns(shard, c)], ig_out_sem.at[c])

    def rep_move(c):
        return pltpu.make_async_remote_copy(
            upd.at[c], got.at[c], rep_send.at[c], rep_recv.at[c],
            device_id=(lax.rem(rep + offset, reps), shard), device_id_type=MESH)

    def nm_store(c):
        return pltpu.make_async_copy(m.at[c], nm_hbm.at[0, rows_of(c)], nm_sem.at[c])

    def part_move(s):
        return pltpu.make_async_remote_copy(
            sent.at[s - 1], part.at[s - 1], part_send.at[s], part_recv.at[s],
            device_id=(rep, behind(s)), device_id_type=MESH)

    barrier = pltpu.get_barrier_semaphore()
    greeted = [(rep, ahead(s)) for s in peers]
    greeted.append((lax.rem(rep + offset, reps), shard))
    if 2 * offset != reps:
        greeted.append((lax.rem(rep + reps - offset, reps), shard))
    for other in greeted:
        pl.semaphore_signal(barrier, inc=1, device_id=other, device_id_type=MESH)
    og_load().start()
    for c in range(chunks):
        load("w", c).start()
    pl.semaphore_wait(barrier, len(greeted))
    for s in peers:
        og_move(s).start()
    for c in range(chunks):
        for s in peers:
            li_move(s, c).start()
    for c in range(chunks):
        for kind in ("li", "m", "v"):
            load(kind, c).start()
    for c in range(chunks):
        ni_load(c).start()

    count = jnp.full((1, width), (step_ref[0] + 1).astype(F32))
    scale_one = learning_rate / (1.0 - jnp.exp(count * math.log(beta_one)))
    scale_two = 1.0 / (1.0 - jnp.exp(count * math.log(beta_two)))

    og_load().wait()
    for s in peers:
        og_move(s).wait_recv()

    @pl.loop(0, chunks)
    def _(c):
        load("w", c).wait()
        ig[c] = lax.dot_general(
            og[...], w[c], (((1,), (1,)), ((), ())), preferred_element_type=F32).astype(BF16)
        ig_store(c).start()

    block = 32

    @pl.loop(0, chunks)
    def _(c):
        for kind in ("li", "m", "v"):
            load(kind, c).wait()
        for s in peers:
            li_move(s, c).wait_recv()
            ni_move(s, c).start()
        grad[...] = lax.dot_general(
            li[c], og[...], (((0,), (0,)), ((), ())), preferred_element_type=F32)

        @pl.loop(0, chunk // block)
        def _(b):
            here = pl.ds(pl.multiple_of(b * block, block), block)
            g = grad[here]
            moment = beta_one * m[c, here] + (1.0 - beta_one) * g
            second = beta_two * v[c, here] + (1.0 - beta_two) * g * g
            m[c, here] = moment
            update = (moment * scale_one) / (jnp.sqrt(second * scale_two) + adam_eps)
            upd[c, here] = (w[c, here].astype(F32) - update).astype(BF16)

        rep_move(c).start()
        nm_store(c).start()

    for c in range(chunks):
        for s in peers:
            ig_move(s, c).start()

    acc[...] = jnp.zeros_like(acc)
    travelling = pl.ds(tokens, (shards - 1) * tokens)

    @pl.loop(0, chunks)
    def _(c):
        ni_load(c).wait()
        for s in peers:
            ni_move(s, c).wait_recv()
        rep_move(c).wait_recv()

        @pl.loop(0, chunk // block)
        def _(b):
            here = pl.ds(pl.multiple_of(b * block, block), block)
            got[c, here] = (0.5 * (upd[c, here].astype(F32) + got[c, here].astype(F32))).astype(BF16)

        if shards > 1:
            acc[travelling] += jnp.dot(ni[c, travelling], got[c], preferred_element_type=F32)

    for s in peers:
        sent[s - 1] = acc[slot(s)].astype(BF16)
        part_move(s).start()

    @pl.loop(0, chunks)
    def _(c):
        acc[slot(0)] += jnp.dot(ni[c, slot(0)], got[c], preferred_element_type=F32)

    total = acc[slot(0)]
    for s in peers:
        part_move(s).wait_recv()
        total = total + part[s - 1].astype(F32)
    no[...] = total.astype(BF16)
    no_store = pltpu.make_async_copy(no, no_hbm, out_sem)
    no_store.start()

    for s in peers:
        og_move(s).wait_send()
        part_move(s).wait_send()
    for c in range(chunks):
        for s in peers:
            li_move(s, c).wait_send()
            ni_move(s, c).wait_send()
            ig_move(s, c).wait_send()
            ig_move(s, c).wait_recv()
        ig_store(c).wait()
        nm_store(c).wait()
        rep_move(c).wait_send()
    no_store.wait()


def step_call(offset, level, reps, shards, operands):
    step_index, weights, first_moment, second_moment, layer_inputs, output_grad, next_inputs = operands
    rows, width = weights.shape[1:]
    tokens, depth = layer_inputs.shape
    chunk = min(256, rows)
    chunks = rows // chunk
    whole = tokens * shards
    dma = pltpu.SemaphoreType.DMA
    anywhere = pl.BlockSpec(memory_space=pl.ANY)
    each, every = dma((shards,)), dma((shards, chunks))
    return pl.pallas_call(
        functools.partial(step_kernel, offset, reps, shards, chunk),
        out_shape=(
            jax.ShapeDtypeStruct((tokens, depth), BF16),
            jax.ShapeDtypeStruct((tokens, width), BF16),
            jax.ShapeDtypeStruct((1, rows, width), F32),
        ),
        in_specs=[pl.BlockSpec(memory_space=pltpu.SMEM)] + [anywhere] * 6,
        out_specs=(anywhere,) * 3,
        scratch_shapes=[
            pltpu.VMEM((chunks, chunk, width), BF16),
            pltpu.VMEM((chunks, chunk, width), F32),
            pltpu.VMEM((chunks, chunk, width), F32),
            pltpu.VMEM((chunks, whole, chunk), BF16),
            pltpu.VMEM((whole, width), BF16),
            pltpu.VMEM((chunks, whole, chunk), BF16),
            pltpu.VMEM((chunk, width), F32),
            pltpu.VMEM((chunks, chunk, width), BF16),
            pltpu.VMEM((chunks, chunk, width), BF16),
            pltpu.VMEM((chunks, whole, chunk), BF16),
            pltpu.VMEM((whole, width), F32),
            pltpu.VMEM((max(shards - 1, 1), tokens, width), BF16),
            pltpu.VMEM((max(shards - 1, 1), tokens, width), BF16),
            pltpu.VMEM((tokens, width), BF16),
            dma((4, chunks)), dma, dma((chunks,)), dma, dma((chunks,)), dma((chunks,)),
            each, each, every, every, every, every, every, every, dma((chunks,)), dma((chunks,)), each, each,
        ],
        compiler_params=pltpu.CompilerParams(
            collective_id=level, has_side_effects=True, vmem_limit_bytes=56 * 1024 * 1024),
        cost_estimate=pl.CostEstimate(
            flops=6 * whole * rows * width, bytes_accessed=12 * 1024 * 1024, transcendentals=rows * width),
        name=f"adam_average_{offset}",
    )(*operands)


def on_device(
    weights, first_moment, second_moment, layer_inputs, output_grad, next_inputs, step_index
):
    reps, shards = lax.axis_size("rep"), lax.axis_size("fsdp")
    levels = reps.bit_length() - 1
    operands = (step_index, weights, first_moment, second_moment, layer_inputs, output_grad, next_inputs)
    branches = [
        lambda *given, level=level: step_call(1 << level, level, reps, shards, given)
        for level in range(levels)
    ]
    return lax.switch(step_index[0] % levels, branches, *operands)


def solution(mesh):
    return jax.shard_map(
        on_device,
        mesh=mesh,
        in_specs=(
            P("rep", "fsdp", None),
            P("rep", "fsdp", None),
            P("rep", "fsdp", None),
            P(("rep", "fsdp"), None),
            P(("rep", "fsdp"), None),
            P(("rep", "fsdp"), None),
            P(),
        ),
        out_specs=(P(("rep", "fsdp"), None), P(("rep", "fsdp"), None), P("rep", "fsdp", None)),
        check_vma=False,
    )
```

```python
import functools
import math

import jax
import jax.numpy as jnp
from jax import lax
from jax.experimental import pallas as pl
from jax.experimental.pallas import tpu as pltpu
from jax.sharding import PartitionSpec as P

learning_rate = 0.004
beta_one = 0.9
beta_two = 0.95
adam_eps = 1e-08
MESH = pl.DeviceIdType.MESH
BF16, F32 = jnp.bfloat16, jnp.float32


def step_kernel(
    offset, reps, shards, chunk, step_ref, w_hbm, m_hbm, v_hbm, li_hbm, og_hbm, ni_hbm,
    ig_hbm, no_hbm, nm_hbm,
    w, m, v, li, og, ni, grad, upd, got, ig, acc, sent, part, no,
    load_sem, og_sem, ni_sem, out_sem, nm_sem, ig_out_sem, og_send, og_recv, li_send, li_recv,
    ni_send, ni_recv, ig_send, ig_recv, rep_send, rep_recv, last_send, last_recv,
    part_send, part_recv,
):
    rep, shard = lax.axis_index("rep"), lax.axis_index("fsdp")
    tokens, width = og_hbm.shape
    rows = w_hbm.shape[1]
    chunks = rows // chunk
    peers = range(1, shards)
    in_flight = min(2, chunks)
    last, piece = chunks - 1, 128
    pieces = width // piece

    def ahead(s):
        return lax.rem(shard + s, shards)

    def behind(s):
        return lax.rem(shard + shards - s, shards)

    def columns(owner, c):
        return pl.ds(pl.multiple_of(owner * rows + c * chunk, chunk), chunk)

    def rows_of(c):
        return pl.ds(pl.multiple_of(c * chunk, chunk), chunk)

    def slot(s):
        return pl.ds(s * tokens, tokens)

    def og_load():
        return pltpu.make_async_copy(og_hbm, og.at[slot(0)], og_sem)

    def load(kind, c):
        source, target = {
            "li": (lambda: li_hbm.at[:, columns(shard, c)], lambda: li.at[c, slot(0)]),
            "w": (lambda: w_hbm.at[0, rows_of(c)], lambda: w.at[c]),
            "m": (lambda: m_hbm.at[0, rows_of(c)], lambda: m.at[c]),
            "v": (lambda: v_hbm.at[0, rows_of(c)], lambda: v.at[c]),
        }[kind]
        return pltpu.make_async_copy(source(), target(), load_sem.at["li w m v".split().index(kind), c])

    def ni_load(c):
        return pltpu.make_async_copy(ni_hbm.at[:, columns(shard, c)], ni.at[c, slot(0)], ni_sem.at[c])

    def og_move(s):
        return pltpu.make_async_remote_copy(
            og_hbm, og.at[slot(s)], og_send.at[s], og_recv.at[s],
            device_id=(rep, ahead(s)), device_id_type=MESH)

    def li_move(s, c):
        return pltpu.make_async_remote_copy(
            li_hbm.at[:, columns(ahead(s), c)], li.at[c, slot(s)], li_send.at[s, c], li_recv.at[s, c],
            device_id=(rep, ahead(s)), device_id_type=MESH)

    def ni_move(s, c):
        return pltpu.make_async_remote_copy(
            ni_hbm.at[:, columns(ahead(s), c)], ni.at[c, slot(s)], ni_send.at[s, c], ni_recv.at[s, c],
            device_id=(rep, ahead(s)), device_id_type=MESH)

    def ig_move(s, c):
        return pltpu.make_async_remote_copy(
            ig.at[c, slot(s)], ig_hbm.at[:, columns(shard, c)], ig_send.at[s, c], ig_recv.at[s, c],
            device_id=(rep, behind(s)), device_id_type=MESH)

    def ig_store(c):
        return pltpu.make_async_copy(ig.at[c, slot(0)], ig_hbm.at[:, columns(shard, c)], ig_out_sem.at[c])

    def rep_move(c):
        return pltpu.make_async_remote_copy(
            upd.at[c], got.at[c], rep_send.at[c], rep_recv.at[c],
            device_id=(lax.rem(rep + offset, reps), shard), device_id_type=MESH)

    def last_move(q):
        across = pl.ds(q * piece, piece)
        return pltpu.make_async_remote_copy(
            upd.at[last, :, across], got.at[last, :, across], last_send.at[q], last_recv.at[q],
            device_id=(lax.rem(rep + offset, reps), shard), device_id_type=MESH)

    def nm_store(c):
        return pltpu.make_async_copy(m.at[c], nm_hbm.at[0, rows_of(c)], nm_sem.at[c])

    def part_move(s, q):
        across = pl.ds(q * piece, piece)
        return pltpu.make_async_remote_copy(
            sent.at[s - 1, :, across], part.at[s - 1, :, across], part_send.at[s, q], part_recv.at[s, q],
            device_id=(rep, behind(s)), device_id_type=MESH)

    barrier = pltpu.get_barrier_semaphore()
    greeted = [(rep, ahead(s)) for s in peers]
    greeted.append((lax.rem(rep + offset, reps), shard))
    if 2 * offset != reps:
        greeted.append((lax.rem(rep + reps - offset, reps), shard))
    for other in greeted:
        pl.semaphore_signal(barrier, inc=1, device_id=other, device_id_type=MESH)
    og_load().start()
    for c in range(chunks):
        load("w", c).start()
    pl.semaphore_wait(barrier, len(greeted))
    for s in peers:
        og_move(s).start()
    for c in range(min(in_flight, chunks)):
        for s in peers:
            li_move(s, c).start()
    for c in range(chunks):
        for kind in ("li", "m", "v"):
            load(kind, c).start()
    for c in range(chunks):
        ni_load(c).start()

    count = jnp.full((1, width), (step_ref[0] + 1).astype(F32))
    scale_one = learning_rate / (1.0 - jnp.exp(count * math.log(beta_one)))
    scale_two = 1.0 / (1.0 - jnp.exp(count * math.log(beta_two)))

    og_load().wait()
    for s in peers:
        og_move(s).wait_recv()

    @pl.loop(0, chunks)
    def _(c):
        load("w", c).wait()
        ig[c] = lax.dot_general(
            og[...], w[c], (((1,), (1,)), ((), ())), preferred_element_type=F32).astype(BF16)
        ig_store(c).start()

    def send_next(turn):
        @pl.when(turn < chunks)
        def _():
            for s in peers:
                li_move(s, turn).start()

        @pl.when(turn >= chunks)
        def _():
            for s in peers:
                ni_move(s, turn - chunks).start()

    block = 32

    @pl.loop(0, chunks)
    def _(c):
        for kind in ("li", "m", "v"):
            load(kind, c).wait()
        for s in peers:
            li_move(s, c).wait_recv()
        send_next(c + in_flight)
        grad[...] = lax.dot_general(
            li[c], og[...], (((0,), (0,)), ((), ())), preferred_element_type=F32)

        @pl.loop(0, chunk // block)
        def _(b):
            here = pl.ds(pl.multiple_of(b * block, block), block)
            g = grad[here]
            moment = beta_one * m[c, here] + (1.0 - beta_one) * g
            second = beta_two * v[c, here] + (1.0 - beta_two) * g * g
            m[c, here] = moment
            update = (moment * scale_one) / (jnp.sqrt(second * scale_two) + adam_eps)
            upd[c, here] = (w[c, here].astype(F32) - update).astype(BF16)

        @pl.when(c < last)
        def _():
            rep_move(c).start()

        nm_store(c).start()

    for q in range(pieces):
        last_move(q).start()

    for c in range(in_flight, chunks):
        for s in peers:
            ni_move(s, c).start()
    for c in range(chunks):
        for s in peers:
            ig_move(s, c).start()

    acc[...] = jnp.zeros_like(acc)
    travelling = pl.ds(tokens, (shards - 1) * tokens)

    @pl.loop(0, last)
    def _(c):
        ni_load(c).wait()
        for s in peers:
            ni_move(s, c).wait_recv()
        rep_move(c).wait_recv()

        @pl.loop(0, chunk // block)
        def _(b):
            here = pl.ds(pl.multiple_of(b * block, block), block)
            got[c, here] = (0.5 * (upd[c, here].astype(F32) + got[c, here].astype(F32))).astype(BF16)

        if shards > 1:
            acc[travelling] += jnp.dot(ni[c, travelling], got[c], preferred_element_type=F32)

    ni_load(last).wait()
    for s in peers:
        ni_move(s, last).wait_recv()
    for q in range(pieces):
        across = slice(q * piece, (q + 1) * piece)
        last_move(q).wait_recv()
        got[last, :, across] = (
            0.5 * (upd[last, :, across].astype(F32) + got[last, :, across].astype(F32))).astype(BF16)
        if shards > 1:
            sums = acc[travelling, across] + jnp.dot(
                ni[last, travelling], got[last, :, across], preferred_element_type=F32)
        for s in peers:
            sent[s - 1, :, across] = sums[(s - 1) * tokens:s * tokens].astype(BF16)
            part_move(s, q).start()

    @pl.loop(0, chunks)
    def _(c):
        acc[slot(0)] += jnp.dot(ni[c, slot(0)], got[c], preferred_element_type=F32)

    total = acc[slot(0)]
    for s in peers:
        for q in range(pieces):
            part_move(s, q).wait_recv()
        total = total + part[s - 1].astype(F32)
    no[...] = total.astype(BF16)
    no_store = pltpu.make_async_copy(no, no_hbm, out_sem)
    no_store.start()

    for s in peers:
        og_move(s).wait_send()
        for q in range(pieces):
            part_move(s, q).wait_send()
    for c in range(chunks):
        for s in peers:
            li_move(s, c).wait_send()
            ni_move(s, c).wait_send()
            ig_move(s, c).wait_send()
            ig_move(s, c).wait_recv()
        ig_store(c).wait()
        nm_store(c).wait()
    for c in range(last):
        rep_move(c).wait_send()
    for q in range(pieces):
        last_move(q).wait_send()
    no_store.wait()


def step_call(offset, level, reps, shards, operands):
    step_index, weights, first_moment, second_moment, layer_inputs, output_grad, next_inputs = operands
    rows, width = weights.shape[1:]
    tokens, depth = layer_inputs.shape
    chunk = min(256, rows)
    chunks = rows // chunk
    whole = tokens * shards
    pieces = width // 128
    dma = pltpu.SemaphoreType.DMA
    anywhere = pl.BlockSpec(memory_space=pl.ANY)
    each, every = dma((shards,)), dma((shards, chunks))
    return pl.pallas_call(
        functools.partial(step_kernel, offset, reps, shards, chunk),
        out_shape=(
            jax.ShapeDtypeStruct((tokens, depth), BF16),
            jax.ShapeDtypeStruct((tokens, width), BF16),
            jax.ShapeDtypeStruct((1, rows, width), F32),
        ),
        in_specs=[pl.BlockSpec(memory_space=pltpu.SMEM)] + [anywhere] * 6,
        out_specs=(anywhere,) * 3,
        scratch_shapes=[
            pltpu.VMEM((chunks, chunk, width), BF16),
            pltpu.VMEM((chunks, chunk, width), F32),
            pltpu.VMEM((chunks, chunk, width), F32),
            pltpu.VMEM((chunks, whole, chunk), BF16),
            pltpu.VMEM((whole, width), BF16),
            pltpu.VMEM((chunks, whole, chunk), BF16),
            pltpu.VMEM((chunk, width), F32),
            pltpu.VMEM((chunks, chunk, width), BF16),
            pltpu.VMEM((chunks, chunk, width), BF16),
            pltpu.VMEM((chunks, whole, chunk), BF16),
            pltpu.VMEM((whole, width), F32),
            pltpu.VMEM((max(shards - 1, 1), tokens, width), BF16),
            pltpu.VMEM((max(shards - 1, 1), tokens, width), BF16),
            pltpu.VMEM((tokens, width), BF16),
            dma((4, chunks)), dma, dma((chunks,)), dma, dma((chunks,)), dma((chunks,)),
            each, each, every, every, every, every, every, every, dma((chunks,)), dma((chunks,)),
            dma((pieces,)), dma((pieces,)), dma((shards, pieces)), dma((shards, pieces)),
        ],
        compiler_params=pltpu.CompilerParams(
            collective_id=level, has_side_effects=True, vmem_limit_bytes=56 * 1024 * 1024),
        cost_estimate=pl.CostEstimate(
            flops=6 * whole * rows * width, bytes_accessed=12 * 1024 * 1024, transcendentals=rows * width),
        name=f"adam_average_{offset}",
    )(*operands)


def on_device(
    weights, first_moment, second_moment, layer_inputs, output_grad, next_inputs, step_index
):
    reps, shards = lax.axis_size("rep"), lax.axis_size("fsdp")
    levels = reps.bit_length() - 1
    operands = (step_index, weights, first_moment, second_moment, layer_inputs, output_grad, next_inputs)
    branches = [
        lambda *given, level=level: step_call(1 << level, level, reps, shards, given)
        for level in range(levels)
    ]
    return lax.switch(step_index[0] % levels, branches, *operands)


def solution(mesh):
    return jax.shard_map(
        on_device,
        mesh=mesh,
        in_specs=(
            P("rep", "fsdp", None),
            P("rep", "fsdp", None),
            P("rep", "fsdp", None),
            P(("rep", "fsdp"), None),
            P(("rep", "fsdp"), None),
            P(("rep", "fsdp"), None),
            P(),
        ),
        out_specs=(P(("rep", "fsdp"), None), P(("rep", "fsdp"), None), P("rep", "fsdp", None)),
        check_vma=False,
    )
```

```python
import functools
import math

import jax
import jax.numpy as jnp
from jax import lax
from jax.experimental import pallas as pl
from jax.experimental.pallas import tpu as pltpu
from jax.sharding import PartitionSpec as P

learning_rate = 0.004
beta_one = 0.9
beta_two = 0.95
adam_eps = 1e-08
MESH = pl.DeviceIdType.MESH
BF16, F32 = jnp.bfloat16, jnp.float32


def step_kernel(
    offset, reps, shards, chunk, step_ref, w_hbm, m_hbm, v_hbm, li_hbm, og_hbm, ni_hbm,
    ig_hbm, no_hbm, nm_hbm,
    w, m, v, li, og, ni, grad, upd, got, ig, acc, sent, part, no,
    load_sem, og_sem, ni_sem, out_sem, nm_sem, ig_out_sem, og_send, og_recv, li_send, li_recv,
    ni_send, ni_recv, ig_send, ig_recv, rep_send, rep_recv, last_send, last_recv,
    part_send, part_recv,
):
    rep, shard = lax.axis_index("rep"), lax.axis_index("fsdp")
    tokens, width = og_hbm.shape
    rows = w_hbm.shape[1]
    chunks = rows // chunk
    peers = range(1, shards)
    in_flight = min(2, chunks)
    last, piece = chunks - 1, 128
    pieces = width // piece

    def ahead(s):
        return lax.rem(shard + s, shards)

    def behind(s):
        return lax.rem(shard + shards - s, shards)

    def columns(owner, c):
        return pl.ds(pl.multiple_of(owner * rows + c * chunk, chunk), chunk)

    def rows_of(c):
        return pl.ds(pl.multiple_of(c * chunk, chunk), chunk)

    def slot(s):
        return pl.ds(s * tokens, tokens)

    def og_load():
        return pltpu.make_async_copy(og_hbm, og.at[slot(0)], og_sem)

    def load(kind, c):
        source, target = {
            "li": (lambda: li_hbm.at[:, columns(shard, c)], lambda: li.at[c, slot(0)]),
            "w": (lambda: w_hbm.at[0, rows_of(c)], lambda: w.at[c]),
            "m": (lambda: m_hbm.at[0, rows_of(c)], lambda: m.at[c]),
            "v": (lambda: v_hbm.at[0, rows_of(c)], lambda: v.at[c]),
        }[kind]
        return pltpu.make_async_copy(source(), target(), load_sem.at["li w m v".split().index(kind), c])

    def ni_load(c):
        return pltpu.make_async_copy(ni_hbm.at[:, columns(shard, c)], ni.at[c, slot(0)], ni_sem.at[c])

    def og_move(s):
        return pltpu.make_async_remote_copy(
            og_hbm, og.at[slot(s)], og_send.at[s], og_recv.at[s],
            device_id=(rep, ahead(s)), device_id_type=MESH)

    def li_move(s, c):
        return pltpu.make_async_remote_copy(
            li_hbm.at[:, columns(ahead(s), c)], li.at[c, slot(s)], li_send.at[s, c], li_recv.at[s, c],
            device_id=(rep, ahead(s)), device_id_type=MESH)

    def ni_move(s, c):
        return pltpu.make_async_remote_copy(
            ni_hbm.at[:, columns(ahead(s), c)], ni.at[c, slot(s)], ni_send.at[s, c], ni_recv.at[s, c],
            device_id=(rep, ahead(s)), device_id_type=MESH)

    def ig_move(s, c):
        return pltpu.make_async_remote_copy(
            ig.at[c, slot(s)], ig_hbm.at[:, columns(shard, c)], ig_send.at[s, c], ig_recv.at[s, c],
            device_id=(rep, behind(s)), device_id_type=MESH)

    def ig_store(c):
        return pltpu.make_async_copy(ig.at[c, slot(0)], ig_hbm.at[:, columns(shard, c)], ig_out_sem.at[c])

    def rep_move(c):
        return pltpu.make_async_remote_copy(
            upd.at[c], got.at[c], rep_send.at[c], rep_recv.at[c],
            device_id=(lax.rem(rep + offset, reps), shard), device_id_type=MESH)

    def last_move(q):
        across = pl.ds(q * piece, piece)
        return pltpu.make_async_remote_copy(
            upd.at[last, :, across], got.at[last, :, across], last_send.at[q], last_recv.at[q],
            device_id=(lax.rem(rep + offset, reps), shard), device_id_type=MESH)

    def nm_store(c):
        return pltpu.make_async_copy(m.at[c], nm_hbm.at[0, rows_of(c)], nm_sem.at[c])

    def part_move(s, q):
        across = pl.ds(q * piece, piece)
        return pltpu.make_async_remote_copy(
            sent.at[s - 1, :, across], part.at[s - 1, :, across], part_send.at[s, q], part_recv.at[s, q],
            device_id=(rep, behind(s)), device_id_type=MESH)

    barrier = pltpu.get_barrier_semaphore()
    greeted = [(rep, ahead(s)) for s in peers]
    greeted.append((lax.rem(rep + offset, reps), shard))
    if 2 * offset != reps:
        greeted.append((lax.rem(rep + reps - offset, reps), shard))
    for other in greeted:
        pl.semaphore_signal(barrier, inc=1, device_id=other, device_id_type=MESH)
    og_load().start()
    for c in range(chunks):
        load("w", c).start()
    pl.semaphore_wait(barrier, len(greeted))
    for s in peers:
        og_move(s).start()
    for c in range(min(in_flight, chunks)):
        for s in peers:
            li_move(s, c).start()
    for c in range(chunks):
        for kind in ("li", "m", "v"):
            load(kind, c).start()
    for c in range(chunks):
        ni_load(c).start()

    count = jnp.full((1, width), (step_ref[0] + 1).astype(F32))
    scale_one = learning_rate / (1.0 - jnp.exp(count * math.log(beta_one)))
    scale_two = 1.0 / (1.0 - jnp.exp(count * math.log(beta_two)))

    og_load().wait()
    for s in peers:
        og_move(s).wait_recv()

    def send_next(turn):
        @pl.when(turn < chunks)
        def _():
            for s in peers:
                li_move(s, turn).start()

        @pl.when(turn >= chunks)
        def _():
            for s in peers:
                ni_move(s, turn - chunks).start()

    block = 64

    @pl.loop(0, chunks)
    def _(c):
        for kind in ("w", "li", "m", "v"):
            load(kind, c).wait()
        for s in peers:
            li_move(s, c).wait_recv()
        send_next(c + in_flight)
        grad[...] = lax.dot_general(
            li[c], og[...], (((0,), (0,)), ((), ())), preferred_element_type=F32)

        @pl.loop(0, chunk // block)
        def _(b):
            here = pl.ds(pl.multiple_of(b * block, block), block)
            g = grad[here]
            moment = beta_one * m[c, here] + (1.0 - beta_one) * g
            second = beta_two * v[c, here] + (1.0 - beta_two) * g * g
            m[c, here] = moment
            update = (moment * scale_one) / (jnp.sqrt(second * scale_two) + adam_eps)
            upd[c, here] = (w[c, here].astype(F32) - update).astype(BF16)

        @pl.when(c < last)
        def _():
            rep_move(c).start()

        @pl.when(c == last)
        def _():
            for q in range(pieces):
                last_move(q).start()

        nm_store(c).start()
        ig[c] = lax.dot_general(
            og[...], w[c], (((1,), (1,)), ((), ())), preferred_element_type=F32).astype(BF16)
        ig_store(c).start()


    for c in range(in_flight, chunks):
        for s in peers:
            ni_move(s, c).start()
    for c in range(chunks):
        for s in peers:
            ig_move(s, c).start()

    acc[...] = jnp.zeros_like(acc)
    travelling = pl.ds(tokens, (shards - 1) * tokens)

    @pl.loop(0, last)
    def _(c):
        ni_load(c).wait()
        for s in peers:
            ni_move(s, c).wait_recv()
        rep_move(c).wait_recv()

        @pl.loop(0, chunk // block)
        def _(b):
            here = pl.ds(pl.multiple_of(b * block, block), block)
            got[c, here] = (0.5 * (upd[c, here].astype(F32) + got[c, here].astype(F32))).astype(BF16)

        acc[...] += jnp.dot(ni[c], got[c], preferred_element_type=F32)

    ni_load(last).wait()
    for s in peers:
        ni_move(s, last).wait_recv()
    for q in range(pieces):
        across = slice(q * piece, (q + 1) * piece)
        last_move(q).wait_recv()
        got[last, :, across] = (
            0.5 * (upd[last, :, across].astype(F32) + got[last, :, across].astype(F32))).astype(BF16)
        if shards > 1:
            sums = acc[travelling, across] + jnp.dot(
                ni[last, travelling], got[last, :, across], preferred_element_type=F32)
        for s in peers:
            sent[s - 1, :, across] = sums[(s - 1) * tokens:s * tokens].astype(BF16)
            part_move(s, q).start()

    total = acc[slot(0)] + jnp.dot(ni[last, slot(0)], got[last], preferred_element_type=F32)
    for s in peers:
        for q in range(pieces):
            part_move(s, q).wait_recv()
        total = total + part[s - 1].astype(F32)
    no[...] = total.astype(BF16)
    no_store = pltpu.make_async_copy(no, no_hbm, out_sem)
    no_store.start()

    for s in peers:
        og_move(s).wait_send()
        for q in range(pieces):
            part_move(s, q).wait_send()
    for c in range(chunks):
        for s in peers:
            li_move(s, c).wait_send()
            ni_move(s, c).wait_send()
            ig_move(s, c).wait_send()
            ig_move(s, c).wait_recv()
        ig_store(c).wait()
        nm_store(c).wait()
    for c in range(last):
        rep_move(c).wait_send()
    for q in range(pieces):
        last_move(q).wait_send()
    no_store.wait()


def step_call(offset, level, reps, shards, operands):
    step_index, weights, first_moment, second_moment, layer_inputs, output_grad, next_inputs = operands
    rows, width = weights.shape[1:]
    tokens, depth = layer_inputs.shape
    chunk = min(256, rows)
    chunks = rows // chunk
    whole = tokens * shards
    pieces = width // 128
    dma = pltpu.SemaphoreType.DMA
    anywhere = pl.BlockSpec(memory_space=pl.ANY)
    each, every = dma((shards,)), dma((shards, chunks))
    return pl.pallas_call(
        functools.partial(step_kernel, offset, reps, shards, chunk),
        out_shape=(
            jax.ShapeDtypeStruct((tokens, depth), BF16),
            jax.ShapeDtypeStruct((tokens, width), BF16),
            jax.ShapeDtypeStruct((1, rows, width), F32),
        ),
        in_specs=[pl.BlockSpec(memory_space=pltpu.SMEM)] + [anywhere] * 6,
        out_specs=(anywhere,) * 3,
        scratch_shapes=[
            pltpu.VMEM((chunks, chunk, width), BF16),
            pltpu.VMEM((chunks, chunk, width), F32),
            pltpu.VMEM((chunks, chunk, width), F32),
            pltpu.VMEM((chunks, whole, chunk), BF16),
            pltpu.VMEM((whole, width), BF16),
            pltpu.VMEM((chunks, whole, chunk), BF16),
            pltpu.VMEM((chunk, width), F32),
            pltpu.VMEM((chunks, chunk, width), BF16),
            pltpu.VMEM((chunks, chunk, width), BF16),
            pltpu.VMEM((chunks, whole, chunk), BF16),
            pltpu.VMEM((whole, width), F32),
            pltpu.VMEM((max(shards - 1, 1), tokens, width), BF16),
            pltpu.VMEM((max(shards - 1, 1), tokens, width), BF16),
            pltpu.VMEM((tokens, width), BF16),
            dma((4, chunks)), dma, dma((chunks,)), dma, dma((chunks,)), dma((chunks,)),
            each, each, every, every, every, every, every, every, dma((chunks,)), dma((chunks,)),
            dma((pieces,)), dma((pieces,)), dma((shards, pieces)), dma((shards, pieces)),
        ],
        compiler_params=pltpu.CompilerParams(
            collective_id=level, has_side_effects=True, vmem_limit_bytes=56 * 1024 * 1024),
        cost_estimate=pl.CostEstimate(
            flops=6 * whole * rows * width, bytes_accessed=12 * 1024 * 1024, transcendentals=rows * width),
        name=f"adam_average_{offset}",
    )(*operands)


def on_device(
    weights, first_moment, second_moment, layer_inputs, output_grad, next_inputs, step_index
):
    reps, shards = lax.axis_size("rep"), lax.axis_size("fsdp")
    levels = reps.bit_length() - 1
    operands = (step_index, weights, first_moment, second_moment, layer_inputs, output_grad, next_inputs)
    branches = [
        lambda *given, level=level: step_call(1 << level, level, reps, shards, given)
        for level in range(levels)
    ]
    return lax.switch(step_index[0] % levels, branches, *operands)


def solution(mesh):
    return jax.shard_map(
        on_device,
        mesh=mesh,
        in_specs=(
            P("rep", "fsdp", None),
            P("rep", "fsdp", None),
            P("rep", "fsdp", None),
            P(("rep", "fsdp"), None),
            P(("rep", "fsdp"), None),
            P(("rep", "fsdp"), None),
            P(),
        ),
        out_specs=(P(("rep", "fsdp"), None), P(("rep", "fsdp"), None), P("rep", "fsdp", None)),
        check_vma=False,
    )
```
